32 devices in a mesh: swath: 2 (over x), tile: 16 (over z, y, core).
Axes of the slice: x: 2, y: 2, z: 4, core: 2. Of those that a mesh axis runs over, the one named last changes fastest.
Arguments:
- traces: bfloat16 [1536, 768, 512], P(('swath', 'tile')), parts along dimension 0, may hold values from -6 to 6
- quality: int32 [1536, 768], P(('swath', 'tile')), parts along dimension 0, may hold values from 0 to 3
Outputs:
- multiples: bfloat16 [1536, 768, 512], P(('swath', 'tile')), parts along dimension 0
The draws below stay inside these ranges and needn't reach their ends.
There are 2 independent parts, one for each index of `swath`. The reference program is written for one: setup_inputs(seed, part) draws one part's arguments, and reference() takes and returns one part's arrays. A program takes and returns all parts, laid end to end along the dimension named above; each array names one. Nothing has to cross between parts.
All inputs are finite; a program needn't handle non-finite values.
Results may differ from the reference program's by a relative error of at most 0.0077.
Values may be sent and summed in bfloat16 or wider, within the bound.
No kernel may reach another device: no remote copies, remote signals or barrier semaphores. Data moves between devices by JAX's collectives and lax.ppermute only.
A program may use at most 320 MiB of HBM per device.

```python
import math
from functools import partial
import jax
import jax.numpy as jnp
from jax import lax

SRC = 768
NT = 512
NF = 64
F_LO = 8
N_TILE = 16


def touch_ends(drawn, stream_key, least, top_value):
    dims = drawn.shape
    spot = [jax.random.randint(jax.random.fold_in(stream_key, axis), (), 0, dims[axis]) for axis in range(len(dims))]
    drawn = drawn.at[tuple(spot)].set(least)
    longest = dims.index(max(dims))
    spot[longest] = (spot[longest] + 1) % dims[longest]
    return drawn.at[tuple(spot)].set(top_value)


def levels(rng, dims, shards, low, largest):
    loudness = 1.0
    for dim, parts in shards:
        heights = jax.random.uniform(jax.random.fold_in(jax.random.fold_in(rng, 6), dim), (parts,), jnp.float32, low / len(shards), largest / len(shards))
        loudness = loudness * jnp.repeat(jnp.exp(heights), dims[dim] // parts).reshape((-1,) + (1,) * (len(dims) - 1 - dim))
    return loudness


def gaussian(key, extent, scale, reach, pieces=(), held_as=jnp.bfloat16):
    entries = jax.random.normal(key, extent, jnp.float32) * scale
    if len(pieces) > 0:
        entries = levels(key, extent, pieces, -0.22, 0.18) * entries
    return jnp.clip(entries, min=-reach, max=reach).astype(held_as)


def setup_inputs(seed: int = 0, part: int = 0) -> dict:
    key_list = jax.random.split(jax.random.key(seed), 3)
    part_splits = jax.random.split(jax.random.fold_in(key_list[2], part), 3)
    traces = gaussian(part_splits[0], (SRC, SRC, NT), 1.0, 6.0, ((0, 16),))
    quality = touch_ends(jax.random.randint(part_splits[1], (SRC, SRC), 0, 4), jax.random.fold_in(part_splits[1], 1), 0, 3).astype(jnp.int32)
    return {"traces": traces, "quality": quality}


def tables():
    bins = F_LO + jnp.arange(NF, dtype=jnp.int32)
    times = jnp.arange(NT, dtype=jnp.int32)
    phase = bins[:, None] * times[None, :] % NT
    angle = phase.astype(jnp.float32) * jnp.float32(2.0 * math.pi / NT)
    cosine = (jnp.cos(angle) / math.sqrt(NT)).astype(jnp.bfloat16)
    sine = (jnp.sin(angle) / math.sqrt(NT)).astype(jnp.bfloat16)
    return jnp.stack([cosine, -sine], axis=1)

def chain(pair, order):
    scale = 1.0 / math.sqrt(order)
    real_part = pair[0]
    imag_part = pair[1]
    scaled_real = real_part * scale
    scaled_imag = imag_part * scale
    operator_block = jnp.concatenate([jnp.concatenate([scaled_real, scaled_imag], 1), jnp.concatenate([-scaled_imag, scaled_real], 1)], 0)
    current = jnp.concatenate([real_part, imag_part], 1)
    first = jnp.dot(current, operator_block, precision=lax.Precision.HIGHEST, preferred_element_type=jnp.float32)
    second = jnp.dot(first, operator_block, precision=lax.Precision.HIGHEST, preferred_element_type=jnp.float32)
    third = jnp.dot(second, operator_block, precision=lax.Precision.HIGHEST, preferred_element_type=jnp.float32)
    predicted = first - second + third
    return jnp.stack([predicted[:, :order], predicted[:, order:]], 0)

def reference(traces, quality):
    forward = tables()
    spectrum = lax.dot_general(forward, traces, (((2,), (2,)), ((), ())), preferred_element_type=jnp.float32)
    weight = (quality + 1).astype(jnp.float32)
    blended = (weight * spectrum + weight.T * jnp.swapaxes(spectrum, 2, 3)) / (weight + weight.T)
    predicted = lax.map(partial(chain, order=SRC), blended)
    inverse = forward.astype(jnp.float32)
    block = SRC // N_TILE
    grouped = jnp.moveaxis(predicted.reshape(NF, 2, SRC // block, block, SRC), 2, 0)

    def back(piece):
        result = lax.dot_general(piece, inverse, (((0, 1), (0, 1)), ((), ())), precision=lax.Precision.HIGHEST, preferred_element_type=jnp.float32)
        return result.astype(jnp.bfloat16)
    return lax.map(back, grouped).reshape(SRC, SRC, NT)
```

```python
import math

import jax
import jax.numpy as jnp
from jax import lax
from jax.sharding import PartitionSpec as P

NT = 512
NF = 64
F_LO = 8


def tables():
    bins = F_LO + jnp.arange(NF, dtype=jnp.int32)
    times = jnp.arange(NT, dtype=jnp.int32)
    phase = bins[:, None] * times[None, :] % NT
    angle = phase.astype(jnp.float32) * jnp.float32(2.0 * math.pi / NT)
    cosine = (jnp.cos(angle) / math.sqrt(NT)).astype(jnp.bfloat16)
    sine = (jnp.sin(angle) / math.sqrt(NT)).astype(jnp.bfloat16)
    return jnp.stack([cosine, -sine], axis=1)


def mm(a, b):
    return jnp.dot(a, b, preferred_element_type=jnp.float32)


def cmul(ar, ai, br, bi):
    return mm(ar, br) - mm(ai, bi), mm(ar, bi) + mm(ai, br)


def chain(yr, yi):
    order = yr.shape[0]
    inv = 1.0 / math.sqrt(order)
    br = yr.astype(jnp.float32) + yr.T.astype(jnp.float32)
    bi = yi.astype(jnp.float32) + yi.T.astype(jnp.float32)
    b16r, b16i = br.astype(jnp.bfloat16), bi.astype(jnp.bfloat16)
    fr, fi = cmul(b16r, b16i, b16r, b16i)
    fr, fi = fr * inv, fi * inv
    gr, gi = (fr - br).astype(jnp.bfloat16), (fi - bi).astype(jnp.bfloat16)
    tr, ti = cmul(fr.astype(jnp.bfloat16), fi.astype(jnp.bfloat16), gr, gi)
    pr, pi = fr + tr * inv, fi + ti * inv
    return pr.astype(jnp.bfloat16), pi.astype(jnp.bfloat16)


def body(traces, quality):
    rows, order = quality.shape
    n = order // rows
    forward = tables()
    weight = (quality + 1).astype(jnp.float32)
    mirror = lax.all_to_all(
        weight.astype(jnp.bfloat16), "tile", split_axis=1, concat_axis=0, tiled=True
    )
    share = weight / (weight + mirror.T.astype(jnp.float32))
    returned = []
    for chunk in range(NF // n):
        part = forward[chunk * n : (chunk + 1) * n]
        spectrum = lax.dot_general(
            part, traces, (((2,), (2,)), ((), ())), preferred_element_type=jnp.float32
        )
        mixed = (share * spectrum).astype(jnp.bfloat16)
        got = lax.all_to_all(mixed, "tile", split_axis=0, concat_axis=0, tiled=True)
        pr, pi = chain(got[:, 0].reshape(order, order), got[:, 1].reshape(order, order))
        back = jnp.stack([pr.reshape(n, rows, order), pi.reshape(n, rows, order)], 1)
        returned.append(
            lax.all_to_all(back, "tile", split_axis=0, concat_axis=0, tiled=True)
        )
    result = lax.dot_general(
        jnp.concatenate(returned, 0),
        forward,
        (((0, 1), (0, 1)), ((), ())),
        preferred_element_type=jnp.float32,
    )
    return result.astype(jnp.bfloat16)


def solution(mesh):
    in_specs = (P(("swath", "tile"), None, None), P(("swath", "tile"), None))
    out_specs = P(("swath", "tile"), None, None)
    return jax.shard_map(body, mesh=mesh, in_specs=in_specs, out_specs=out_specs, check_vma=False)
```

```python
import functools
import math

import jax
import jax.numpy as jnp
from jax import lax
from jax.experimental import pallas as pl
from jax.experimental.pallas import tpu as pltpu
from jax.sharding import PartitionSpec as P

NT = 512
NF = 64
F_LO = 8
TILE = 16


def tables():
    bins = F_LO + jnp.arange(NF, dtype=jnp.int32)
    times = jnp.arange(NT, dtype=jnp.int32)
    phase = bins[:, None] * times[None, :] % NT
    angle = phase.astype(jnp.float32) * jnp.float32(2.0 * math.pi / NT)
    cosine = (jnp.cos(angle) / math.sqrt(NT)).astype(jnp.bfloat16)
    sine = (jnp.sin(angle) / math.sqrt(NT)).astype(jnp.bfloat16)
    return jnp.stack([cosine, -sine], axis=1)


def mm(a, b):
    return jnp.dot(a, b, preferred_element_type=jnp.float32)


def kept(i, j, s, r, group):
    diff = i ^ j
    part = (r > s).astype(jnp.int32)
    bit = 1
    while bit < group:
        part = jnp.where(diff >= bit, (i // bit) % 2, part)
        bit *= 2
    return part == 1


def pair_mask(rows, group, first_row, count):
    s = lax.broadcasted_iota(jnp.int32, (count, rows * group), 0) + first_row
    r = lax.broadcasted_iota(jnp.int32, (count, rows * group), 1)
    return kept(s // rows, r // rows, s, r, group), s == r


def chain_kernel(rows, slot, packed_in, packed_out, *refs):
    count = 4 if packed_in else 1
    ins, ratio, out, (br, bi, fr, fi) = refs[:count], refs[count], refs[count + 1], refs[count + 2 :]
    order = br.shape[0]
    half = order // 2
    n = order // rows
    inv = 1.0 / math.sqrt(order)
    f32, b16 = jnp.float32, jnp.bfloat16
    if packed_in or packed_out:
        mask, diag = pair_mask(rows, n // 2, 0, half)
    if packed_in:
        re, im, mix, extra = ins
        for ref, b in ((re, br), (im, bi)):
            upper = ref[: n // 2].reshape(half, half).astype(f32)
            lower = ref[n // 2 :].reshape(half, half).astype(f32)
            cross = (upper + lower.T) * ratio[:half, half:]
            b[:half, half:] = cross.astype(b16)
            b[half:, :half] = cross.T.astype(b16)
        for h in range(2):
            pick = slice(h * half, (h + 1) * half)
            both = mix[h * (n // 2) : (h + 1) * (n // 2)].reshape(half, half).astype(f32)
            tr = jnp.where(mask, 0.0, both)
            br[pick, pick] = ((tr + tr.T) * ratio[pick, pick]).astype(b16)
            line = jnp.sum(
                extra[h * (n // 2) : (h + 1) * (n // 2), slot : slot + 1].astype(f32), axis=0
            )
            ti = jnp.where(mask, both, 0.0)
            ti = ti + ti.T + jnp.where(diag, 2.0 * line, 0.0)
            bi[pick, pick] = (ti * ratio[pick, pick]).astype(b16)
    else:
        for c, b in ((0, br), (1, bi)):
            y = ins[0][:, c].reshape(order, order).astype(f32)
            b[...] = ((y + y.T) * ratio[...]).astype(b16)
    step = 256 if order % 256 == 0 else order
    for t in range(0, order, step):
        ar, ai = br[t : t + step], bi[t : t + step]
        fr[t : t + step] = (mm(ar, br[...]) - mm(ai, bi[...])) * inv
        fi[t : t + step] = (mm(ar, bi[...]) + mm(ai, br[...])) * inv
    gr = (fr[...] - br[...].astype(f32)).astype(b16)
    gi = (fi[...] - bi[...].astype(f32)).astype(b16)
    br[...] = gr
    bi[...] = gi
    for t in range(0, order, step):
        cr, ci = fr[t : t + step], fi[t : t + step]
        ar, ai = cr.astype(b16), ci.astype(b16)
        pr = cr + (mm(ar, br[...]) - mm(ai, bi[...])) * inv
        pi = ci + (mm(ar, bi[...]) + mm(ai, br[...])) * inv
        fr[t : t + step] = pr
        fi[t : t + step] = pi
    if packed_out:
        out[:, 3 * rows :] = jnp.zeros((n, TILE, half), b16)
        for h in range(2):
            own = slice(h * half, (h + 1) * half)
            other = slice((1 - h) * half, (2 - h) * half)
            dst = slice(h * (n // 2), (h + 1) * (n // 2))
            shape = (n // 2, rows, half)
            out[dst, :rows] = fr[own, other].astype(b16).reshape(shape)
            out[dst, rows : 2 * rows] = fi[own, other].astype(b16).reshape(shape)
            pr, pi = fr[own, own], fi[own, own]
            out[dst, 2 * rows : 3 * rows] = jnp.where(mask, pi, pr).astype(b16).reshape(shape)
            line = jnp.sum(jnp.where(diag, pi, 0.0), axis=0, keepdims=True)
            tile = jnp.where(
                lax.broadcasted_iota(jnp.int32, (TILE, half), 0) == slot,
                jnp.broadcast_to(line, (TILE, half)),
                0.0,
            ).astype(b16)
            out[dst, 3 * rows :] = jnp.broadcast_to(tile[None], (n // 2, TILE, half))
    else:
        out[:, 0] = fr[...].astype(b16).reshape(n, rows, order)
        out[:, 1] = fi[...].astype(b16).reshape(n, rows, order)


def chain(got, ratio, rows, order, slot_in, total_in, slot_out, packed_out):
    n, half = order // rows, order // 2
    packed_in = total_in > 0
    slot = slot_in if packed_in else slot_out
    if packed_in:
        specs = [
            pl.BlockSpec((n, rows, half), functools.partial(lambda b, i: (0, b, 0), 3 * slot_in + c))
            for c in range(3)
        ]
        last = 3 * rows * total_in // TILE
        specs.append(pl.BlockSpec((n, TILE, half), lambda i: (0, last, 0)))
        args = [got] * 4 + [ratio]
    else:
        specs = [pl.BlockSpec((n, 2, rows, order), lambda i: (0, 0, 0, 0))]
        args = [got, ratio]
    specs.append(pl.BlockSpec((order, order), lambda i: (0, 0)))
    shape = (n, 3 * rows + TILE, half) if packed_out else (n, 2, rows, order)
    return pl.pallas_call(
        functools.partial(chain_kernel, rows, slot, packed_in, packed_out),
        out_shape=jax.ShapeDtypeStruct(shape, jnp.bfloat16),
        grid=(1,),
        in_specs=specs,
        out_specs=pl.BlockSpec(shape, lambda i: (0,) * len(shape)),
        scratch_shapes=[
            pltpu.VMEM((order, order), jnp.bfloat16),
            pltpu.VMEM((order, order), jnp.bfloat16),
            pltpu.VMEM((order, order), jnp.float32),
            pltpu.VMEM((order, order), jnp.float32),
        ],
        compiler_params=pltpu.CompilerParams(vmem_limit_bytes=48 * 1024 * 1024),
        cost_estimate=pl.CostEstimate(
            flops=16 * order**3, bytes_accessed=8 * order * order, transcendentals=0
        ),
    )(*args)


def side(ref, upper, inside):
    half = ref.shape[-1] // 2
    low, high = ref[..., :half].astype(jnp.float32), ref[..., half:].astype(jnp.float32)
    return jnp.where(upper == inside, low, high)


def give_kernel(rows, group, whole, where_ref, x, *outs):
    me, upper = where_ref[0], where_ref[1] == 1
    turned = outs[-1]
    n, half = 2 * group, rows * group
    if whole:
        mask, diag = pair_mask(rows, group, me * rows, rows)
        re, im = side(x.at[:, 0, 0], upper, True), side(x.at[:, 0, 1], upper, True)
        block = jnp.where(diag[None], 0.0, jnp.where(mask[None], re, im))
    else:
        block = x[...].astype(jnp.float32)
    turned[...] = block.reshape(n * rows, half).T.astype(jnp.bfloat16).reshape(group, rows, n * rows)
    for m in range(group):
        outs[m][...] = turned[me ^ m]


def give(x, where, rows, group, count, whole):
    n, half = 2 * group, rows * group
    if whole:
        spec = pl.BlockSpec((n, 1, 2, rows, 2 * half), lambda f, w: (0, f + 1, 0, 0, 0))
    else:
        spec = pl.BlockSpec((n, rows, half), lambda f, w: (0, 3 * f + 2, 0))
    return pl.pallas_call(
        functools.partial(give_kernel, rows, group, whole),
        out_shape=[jax.ShapeDtypeStruct((rows, count * n * rows), jnp.bfloat16)] * group,
        grid_spec=pltpu.PrefetchScalarGridSpec(
            num_scalar_prefetch=1,
            grid=(count,),
            in_specs=[spec],
            out_specs=[pl.BlockSpec((rows, n * rows), lambda f, w: (0, f))] * group,
            scratch_shapes=[pltpu.VMEM((group, rows, n * rows), jnp.bfloat16)],
        ),
        compiler_params=pltpu.CompilerParams(vmem_limit_bytes=48 * 1024 * 1024),
        cost_estimate=pl.CostEstimate(
            flops=0, bytes_accessed=count * 16 * rows * n * half, transcendentals=0
        ),
    )(where, x)


def place(pieces, me, rows, group, spread, other):
    for m in range(group):
        spread[me ^ m] = pieces[m][...].astype(jnp.float32)
    for j in range(group):
        for d in range(2 * group):
            other[d, :, j * rows : (j + 1) * rows] = spread[j, :, d * rows : (d + 1) * rows]


def pack_kernel(rows, group, count, where_ref, x, *refs):
    me, upper = where_ref[0], where_ref[1] == 1
    pieces, out, (spread, other) = refs[:group], refs[group], refs[group + 1 :]
    n, half = 2 * group, rows * group
    b16 = jnp.bfloat16
    f = pl.program_id(0)
    place(pieces, me, rows, group, spread, other)
    mask, diag = pair_mask(rows, group, me * rows, rows)
    base = pl.multiple_of(f * 3 * rows, 16)
    for c in range(2):
        out[:, pl.ds(base + c * rows, rows)] = side(x.at[:, 0, c], upper, False).astype(b16)
    re, im = side(x.at[:, 0, 0], upper, True), side(x.at[:, 0, 1], upper, True)
    keep = jnp.where(mask[None], im, re) + other[...]
    out[:, pl.ds(base + 2 * rows, rows)] = keep.astype(b16)
    line = jnp.sum(jnp.where(diag[None], im, 0.0), axis=1, keepdims=True)
    slot = lax.broadcasted_iota(jnp.int32, (n, TILE, half), 1) == f
    tile = jnp.where(slot, jnp.broadcast_to(line, (n, TILE, half)), 0.0)

    @pl.when(f == 0)
    def _():
        out[:, count * 3 * rows :] = jnp.zeros((n, TILE, half), b16)

    old = out[:, count * 3 * rows :].astype(jnp.float32)
    out[:, count * 3 * rows :] = (old + tile).astype(b16)


def pack(x, pieces, where, rows, group, count):
    n, half = 2 * group, rows * group
    shape = (n, count * 3 * rows + TILE, half)
    return pl.pallas_call(
        functools.partial(pack_kernel, rows, group, count),
        out_shape=jax.ShapeDtypeStruct(shape, jnp.bfloat16),
        grid_spec=pltpu.PrefetchScalarGridSpec(
            num_scalar_prefetch=1,
            grid=(count,),
            in_specs=[pl.BlockSpec((n, 1, 2, rows, 2 * half), lambda f, w: (0, f + 1, 0, 0, 0))]
            + [pl.BlockSpec((rows, n * rows), lambda f, w: (0, f))] * group,
            out_specs=pl.BlockSpec(shape, lambda f, w: (0, 0, 0)),
            scratch_shapes=[
                pltpu.VMEM((group, rows, n * rows), jnp.float32),
                pltpu.VMEM((n, rows, half), jnp.float32),
            ],
        ),
        compiler_params=pltpu.CompilerParams(vmem_limit_bytes=48 * 1024 * 1024),
        cost_estimate=pl.CostEstimate(
            flops=0, bytes_accessed=count * 20 * rows * n * half, transcendentals=0
        ),
    )(where, x, *pieces)


def unpack_kernel(rows, group, where_ref, re_ref, im_ref, mix_ref, tile_ref, *refs):
    me, upper = where_ref[0], where_ref[1] == 1
    pieces, out, (spread, other) = refs[:group], refs[group], refs[group + 1 :]
    n, half = 2 * group, rows * group
    b16, f32 = jnp.bfloat16, jnp.float32
    f = pl.program_id(0)
    place(pieces, me, rows, group, spread, other)
    mask, diag = pair_mask(rows, group, me * rows, rows)
    slot = lax.broadcasted_iota(jnp.int32, (n, TILE, half), 1) == f
    line = jnp.sum(jnp.where(slot, tile_ref[...].astype(f32), 0.0), axis=1, keepdims=True)
    mix, rest = mix_ref[...].astype(f32), other[...]
    for c, ref in ((0, re_ref), (1, im_ref)):
        if c == 0:
            inner = jnp.where(mask[None], rest, mix)
        else:
            inner = jnp.where(diag[None], line, jnp.where(mask[None], mix, rest))
        outer = ref[...].astype(f32)
        out[:, c, :, :half] = jnp.where(upper, inner, outer).astype(b16)
        out[:, c, :, half:] = jnp.where(upper, outer, inner).astype(b16)


def unpack(back, pieces, where, rows, group, count):
    n, half = 2 * group, rows * group
    last = 3 * rows * count // TILE
    return pl.pallas_call(
        functools.partial(unpack_kernel, rows, group),
        out_shape=jax.ShapeDtypeStruct((count * n, 2, rows, 2 * half), jnp.bfloat16),
        grid_spec=pltpu.PrefetchScalarGridSpec(
            num_scalar_prefetch=1,
            grid=(count,),
            in_specs=[
                pl.BlockSpec((n, rows, half), functools.partial(lambda c, f, w: (0, 3 * f + c, 0), c))
                for c in range(3)
            ]
            + [pl.BlockSpec((n, TILE, half), lambda f, w: (0, last, 0))]
            + [pl.BlockSpec((rows, n * rows), lambda f, w: (0, f))] * group,
            out_specs=pl.BlockSpec((n, 2, rows, 2 * half), lambda f, w: (f, 0, 0, 0)),
            scratch_shapes=[
                pltpu.VMEM((group, rows, n * rows), jnp.float32),
                pltpu.VMEM((n, rows, half), jnp.float32),
            ],
        ),
        compiler_params=pltpu.CompilerParams(vmem_limit_bytes=48 * 1024 * 1024),
        cost_estimate=pl.CostEstimate(
            flops=0, bytes_accessed=count * 20 * rows * n * half, transcendentals=0
        ),
    )(where, *[back] * 4, *pieces)


def swap(pieces, n):
    return list(pieces[:1]) + [
        lax.ppermute(piece, "tile", [(i, i ^ m) for i in range(n)])
        for m, piece in enumerate(pieces)
        if m
    ]


def a2a(x):
    return lax.all_to_all(x, "tile", split_axis=0, concat_axis=0, tiled=True)


def spectrum_of(part, traces):
    return lax.dot_general(
        part, traces, (((part.ndim - 1,), (2,)), ((), ())), preferred_element_type=jnp.float32
    )


def generic(traces, weight, forward, n):
    rows, order = weight.shape
    mirror = lax.all_to_all(
        weight.astype(jnp.bfloat16), "tile", split_axis=1, concat_axis=0, tiled=True
    )
    share = weight / (weight + mirror.T.astype(jnp.float32))
    returned = []
    for chunk in range(NF // n):
        part = forward[chunk * n : (chunk + 1) * n]
        got = a2a((share * spectrum_of(part, traces)).astype(jnp.bfloat16))
        y = [got[:, c].reshape(order, order).astype(jnp.float32) for c in range(2)]
        br, bi = ((v + v.T).astype(jnp.bfloat16) for v in y)
        inv = 1.0 / math.sqrt(order)
        fr, fi = (mm(br, br) - mm(bi, bi)) * inv, (mm(br, bi) + mm(bi, br)) * inv
        gr, gi = (fr - br).astype(jnp.bfloat16), (fi - bi).astype(jnp.bfloat16)
        ar, ai = fr.astype(jnp.bfloat16), fi.astype(jnp.bfloat16)
        parts = [
            fr + (mm(ar, gr) - mm(ai, gi)) * inv,
            fi + (mm(ar, gi) + mm(ai, gr)) * inv,
        ]
        back = jnp.stack([v.astype(jnp.bfloat16).reshape(n, rows, order) for v in parts], 1)
        returned.append(a2a(back))
    return jnp.concatenate(returned, 0)


def pipelined(traces, weight, forward, n):
    order = traces.shape[1]
    rows = traces.shape[0]
    half, group = order // 2, n // 2
    per = NF // n
    b16 = jnp.bfloat16
    index = lax.axis_index("tile")
    where = jnp.stack([index % group, (index < group).astype(jnp.int32)])

    every = lax.all_gather(weight.astype(b16), "tile", axis=0, tiled=True).astype(jnp.float32)
    ratio = 1.0 / (every + every.T)
    part = forward.reshape(per, n, 2, NT).transpose(1, 0, 2, 3)
    mixed = (weight * spectrum_of(part, traces)).astype(b16)
    mixed, ratio = lax.optimization_barrier((mixed, ratio))

    whole = a2a(mixed[:, 0])
    rest = per - 1
    pieces = swap(give(mixed, where, rows, group, rest, True), n)
    got = a2a(pack(mixed, pieces, where, rows, group, rest))

    answers = [chain(whole, ratio, rows, order, 0, 0, 0, True)]
    for f in range(rest):
        answers.append(chain(got, ratio, rows, order, f, rest, f, f < rest - 1))

    def bring(fs):
        count = len(fs)
        if count > 1:
            tile = sum(answers[f][:, 3 * rows :] for f in fs)
            sent = jnp.concatenate([answers[f][:, : 3 * rows] for f in fs] + [tile], 1)
        else:
            sent = answers[fs[0]]
        back = a2a(sent)
        return back, swap(give(back, where, rows, group, count, False), n)

    early = bring([0])
    later = bring(list(range(1, per - 1)))
    early, final = lax.optimization_barrier((early, answers[-1]))
    returned = [
        unpack(*early, where, rows, group, 1),
        unpack(*later, where, rows, group, per - 2),
        a2a(final),
    ]
    return jnp.concatenate(returned, 0)


def body(traces, quality):
    rows, order = quality.shape
    n = order // rows
    forward = tables()
    weight = (quality + 1).astype(jnp.float32)
    if rows % 16 == 0 and order % 256 == 0 and n & (n - 1) == 0 and NF // n >= 3:
        returned = pipelined(traces, weight, forward, n)
    else:
        returned = generic(traces, weight, forward, n)
    result = lax.dot_general(
        returned, forward, (((0, 1), (0, 1)), ((), ())), preferred_element_type=jnp.float32
    )
    return result.astype(jnp.bfloat16)


def solution(mesh):
    in_specs = (P(("swath", "tile"), None, None), P(("swath", "tile"), None))
    out_specs = P(("swath", "tile"), None, None)
    return jax.shard_map(body, mesh=mesh, in_specs=in_specs, out_specs=out_specs, check_vma=False)
```

```python
import functools
import math

import jax
import jax.numpy as jnp
from jax import lax
from jax.experimental import pallas as pl
from jax.experimental.pallas import tpu as pltpu
from jax.sharding import PartitionSpec as P

NT = 512
NF = 64
F_LO = 8
TILE = 16


def tables():
    bins = F_LO + jnp.arange(NF, dtype=jnp.int32)
    times = jnp.arange(NT, dtype=jnp.int32)
    phase = bins[:, None] * times[None, :] % NT
    angle = phase.astype(jnp.float32) * jnp.float32(2.0 * math.pi / NT)
    cosine = (jnp.cos(angle) / math.sqrt(NT)).astype(jnp.bfloat16)
    sine = (jnp.sin(angle) / math.sqrt(NT)).astype(jnp.bfloat16)
    return jnp.stack([cosine, -sine], axis=1)


def mm(a, b):
    return jnp.dot(a, b, preferred_element_type=jnp.float32)


def kept(i, j, s, r, group):
    diff = i ^ j
    part = (r > s).astype(jnp.int32)
    bit = 1
    while bit < group:
        part = jnp.where(diff >= bit, (i // bit) % 2, part)
        bit *= 2
    return part == 1


def pair_mask(rows, group, first_row, count):
    s = lax.broadcasted_iota(jnp.int32, (count, rows * group), 0) + first_row
    r = lax.broadcasted_iota(jnp.int32, (count, rows * group), 1)
    return kept(s // rows, r // rows, s, r, group), s == r


def chain_kernel(rows, slot_in, slot_out, packed_in, packed_out, *refs):
    count = 4 if packed_in else 1
    ins, ratio, out, (br, bi, fr, fi) = refs[:count], refs[count], refs[count + 1], refs[count + 2 :]
    order = br.shape[0]
    half = order // 2
    n = order // rows
    inv = 1.0 / math.sqrt(order)
    f32, b16 = jnp.float32, jnp.bfloat16
    if packed_in or packed_out:
        mask, diag = pair_mask(rows, n // 2, 0, half)
    if packed_in:
        re, im, mix, extra = ins
        for ref, b in ((re, br), (im, bi)):
            upper = ref[: n // 2].reshape(half, half).astype(f32)
            lower = ref[n // 2 :].reshape(half, half).astype(f32)
            cross = (upper + lower.T) * ratio[:half, half:]
            b[:half, half:] = cross.astype(b16)
            b[half:, :half] = cross.T.astype(b16)
        for h in range(2):
            pick = slice(h * half, (h + 1) * half)
            both = mix[h * (n // 2) : (h + 1) * (n // 2)].reshape(half, half).astype(f32)
            tr = jnp.where(mask, 0.0, both)
            br[pick, pick] = ((tr + tr.T) * ratio[pick, pick]).astype(b16)
            line = jnp.sum(
                extra[h * (n // 2) : (h + 1) * (n // 2), slot_in : slot_in + 1].astype(f32), axis=0
            )
            ti = jnp.where(mask, both, 0.0)
            ti = ti + ti.T + jnp.where(diag, 2.0 * line, 0.0)
            bi[pick, pick] = (ti * ratio[pick, pick]).astype(b16)
    else:
        for c, b in ((0, br), (1, bi)):
            y = ins[0][:, 0, c].reshape(order, order).astype(f32)
            b[...] = ((y + y.T) * ratio[...]).astype(b16)
    step = 256 if order % 256 == 0 else order
    for t in range(0, order, step):
        ar, ai = br[t : t + step], bi[t : t + step]
        fr[t : t + step] = (mm(ar, br[...]) - mm(ai, bi[...])) * inv
        fi[t : t + step] = (mm(ar, bi[...]) + mm(ai, br[...])) * inv
    gr = (fr[...] - br[...].astype(f32)).astype(b16)
    gi = (fi[...] - bi[...].astype(f32)).astype(b16)
    br[...] = gr
    bi[...] = gi
    for t in range(0, order, step):
        cr, ci = fr[t : t + step], fi[t : t + step]
        ar, ai = cr.astype(b16), ci.astype(b16)
        pr = cr + (mm(ar, br[...]) - mm(ai, bi[...])) * inv
        pi = ci + (mm(ar, bi[...]) + mm(ai, br[...])) * inv
        fr[t : t + step] = pr
        fi[t : t + step] = pi
    if packed_out:
        out[:, 3 * rows :] = jnp.zeros((n, TILE, half), b16)
        for h in range(2):
            own = slice(h * half, (h + 1) * half)
            other = slice((1 - h) * half, (2 - h) * half)
            dst = slice(h * (n // 2), (h + 1) * (n // 2))
            shape = (n // 2, rows, half)
            out[dst, :rows] = fr[own, other].astype(b16).reshape(shape)
            out[dst, rows : 2 * rows] = fi[own, other].astype(b16).reshape(shape)
            pr, pi = fr[own, own], fi[own, own]
            out[dst, 2 * rows : 3 * rows] = jnp.where(mask, pi, pr).astype(b16).reshape(shape)
            line = jnp.sum(jnp.where(diag, pi, 0.0), axis=0, keepdims=True)
            tile = jnp.where(
                lax.broadcasted_iota(jnp.int32, (TILE, half), 0) == slot_out,
                jnp.broadcast_to(line, (TILE, half)),
                0.0,
            ).astype(b16)
            out[dst, 3 * rows :] = jnp.broadcast_to(tile[None], (n // 2, TILE, half))
    else:
        out[:, 0] = fr[...].astype(b16).reshape(n, rows, order)
        out[:, 1] = fi[...].astype(b16).reshape(n, rows, order)


def chain(got, ratio, rows, order, slot_in, total_in, slot_out, packed_out):
    n, half = order // rows, order // 2
    packed_in = total_in > 0
    if packed_in:
        specs = [
            pl.BlockSpec((n, rows, half), functools.partial(lambda b, i: (0, b, 0), 3 * slot_in + c))
            for c in range(3)
        ]
        last = 3 * rows * total_in // TILE
        specs.append(pl.BlockSpec((n, TILE, half), lambda i: (0, last, 0)))
        args = [got] * 4 + [ratio]
    else:
        specs = [pl.BlockSpec((n, 1, 2, rows, order), lambda i: (0, slot_in, 0, 0, 0))]
        args = [got, ratio]
    specs.append(pl.BlockSpec((order, order), lambda i: (0, 0)))
    shape = (n, 3 * rows + TILE, half) if packed_out else (n, 2, rows, order)
    return pl.pallas_call(
        functools.partial(chain_kernel, rows, slot_in, slot_out, packed_in, packed_out),
        out_shape=jax.ShapeDtypeStruct(shape, jnp.bfloat16),
        grid=(1,),
        in_specs=specs,
        out_specs=pl.BlockSpec(shape, lambda i: (0,) * len(shape)),
        scratch_shapes=[
            pltpu.VMEM((order, order), jnp.bfloat16),
            pltpu.VMEM((order, order), jnp.bfloat16),
            pltpu.VMEM((order, order), jnp.float32),
            pltpu.VMEM((order, order), jnp.float32),
        ],
        compiler_params=pltpu.CompilerParams(vmem_limit_bytes=48 * 1024 * 1024),
        cost_estimate=pl.CostEstimate(
            flops=16 * order**3, bytes_accessed=8 * order * order, transcendentals=0
        ),
    )(*args)


def dft_kernel(first, table, weight, traces, head, tail, turn):
    rb, cb = traces.shape[:2]
    count = table.shape[0]
    b16 = jnp.bfloat16
    for s in range(rb):
        lines = lax.dot_general(
            traces[s], table[...], (((1,), (1,)), ((), ())), preferred_element_type=jnp.float32
        ).T
        lines = lines * weight[s : s + 1]
        for c in range(cb // 128):
            turn[c, pl.ds(s, count, stride=rb), :] = lines[:, c * 128 : (c + 1) * 128]
    for c in range(cb // 128):
        pick = slice(c * 128, (c + 1) * 128)
        head[:, :, pick] = turn[c, : first * rb].reshape(first, rb, 128).astype(b16)
        tail[:, :, pick] = turn[c, first * rb :].reshape(count - first, rb, 128).astype(b16)


def dft(traces, weight, table, first):
    rows, order, nt = traces.shape
    count = table.shape[0]
    rb, cb = 16, 384 if order % 384 == 0 else 128
    return pl.pallas_call(
        functools.partial(dft_kernel, first),
        out_shape=[
            jax.ShapeDtypeStruct((first, rows, order), jnp.bfloat16),
            jax.ShapeDtypeStruct((count - first, rows, order), jnp.bfloat16),
        ],
        grid=(rows // rb, order // cb),
        in_specs=[
            pl.BlockSpec((count, nt), lambda i, j: (0, 0)),
            pl.BlockSpec((rb, cb), lambda i, j: (i, j)),
            pl.BlockSpec((rb, cb, nt), lambda i, j: (i, j, 0)),
        ],
        out_specs=[
            pl.BlockSpec((first, rb, cb), lambda i, j: (0, i, j)),
            pl.BlockSpec((count - first, rb, cb), lambda i, j: (0, i, j)),
        ],
        scratch_shapes=[pltpu.VMEM((cb // 128, count * rb, 128), jnp.float32)],
        compiler_params=pltpu.CompilerParams(vmem_limit_bytes=52 * 1024 * 1024),
        cost_estimate=pl.CostEstimate(
            flops=4 * count * rows * order * nt,
            bytes_accessed=2 * rows * order * (nt + count),
            transcendentals=0,
        ),
    )(table, weight, traces)


def idft_kernel(parts, table, *refs):
    ins, out, turn = refs[:parts], refs[parts], refs[parts + 1]
    rb, cb = out.shape[:2]
    count = table.shape[0]
    at = 0
    for ref in ins:
        size = ref.shape[0] * rb
        for c in range(cb // 128):
            piece = ref[:, :, c * 128 : (c + 1) * 128].astype(jnp.float32)
            turn[c, at : at + size] = piece.reshape(size, 128)
        at += size
    for s in range(rb):
        for c in range(cb // 128):
            lines = turn[c, pl.ds(s, count, stride=rb), :].astype(jnp.bfloat16)
            samples = lax.dot_general(
                lines, table[...], (((0,), (0,)), ((), ())), preferred_element_type=jnp.float32
            )
            out[s, c * 128 : (c + 1) * 128] = samples.astype(jnp.bfloat16)


def idft(pieces, table):
    count, nt = table.shape
    rows, order = pieces[0].shape[1:]
    rb, cb = 16, 384 if order % 384 == 0 else 128
    return pl.pallas_call(
        functools.partial(idft_kernel, len(pieces)),
        out_shape=jax.ShapeDtypeStruct((rows, order, nt), jnp.bfloat16),
        grid=(rows // rb, order // cb),
        in_specs=[pl.BlockSpec((count, nt), lambda i, j: (0, 0))]
        + [pl.BlockSpec((piece.shape[0], rb, cb), lambda i, j: (0, i, j)) for piece in pieces],
        out_specs=pl.BlockSpec((rb, cb, nt), lambda i, j: (i, j, 0)),
        scratch_shapes=[pltpu.VMEM((cb // 128, count * rb, 128), jnp.float32)],
        compiler_params=pltpu.CompilerParams(vmem_limit_bytes=52 * 1024 * 1024),
        cost_estimate=pl.CostEstimate(
            flops=4 * count * rows * order * nt,
            bytes_accessed=2 * rows * order * (nt + count),
            transcendentals=0,
        ),
    )(table, *pieces)


def side(ref, upper, inside):
    half = ref.shape[-1] // 2
    low, high = ref[..., :half].astype(jnp.float32), ref[..., half:].astype(jnp.float32)
    return jnp.where(upper == inside, low, high)


def give_kernel(rows, group, whole, where_ref, x, *outs):
    me, upper = where_ref[0], where_ref[1] == 1
    turned = outs[-1]
    n, half = 2 * group, rows * group
    if whole:
        mask, diag = pair_mask(rows, group, me * rows, rows)
        re, im = side(x.at[0, :, 0], upper, True), side(x.at[0, :, 1], upper, True)
        block = jnp.where(diag[None], 0.0, jnp.where(mask[None], re, im))
    else:
        block = x[...].astype(jnp.float32)
    turned[...] = block.reshape(n * rows, half).T.astype(jnp.bfloat16).reshape(group, rows, n * rows)
    for m in range(group):
        outs[m][...] = turned[me ^ m]


def give(x, where, rows, group, first, count, whole):
    n, half = 2 * group, rows * group
    if whole:
        spec = pl.BlockSpec((1, n, 2, rows, 2 * half), lambda f, w: (f + first, 0, 0, 0, 0))
    else:
        spec = pl.BlockSpec((n, rows, half), lambda f, w: (0, 3 * f + 2, 0))
    return pl.pallas_call(
        functools.partial(give_kernel, rows, group, whole),
        out_shape=[jax.ShapeDtypeStruct((rows, count * n * rows), jnp.bfloat16)] * group,
        grid_spec=pltpu.PrefetchScalarGridSpec(
            num_scalar_prefetch=1,
            grid=(count,),
            in_specs=[spec],
            out_specs=[pl.BlockSpec((rows, n * rows), lambda f, w: (0, f))] * group,
            scratch_shapes=[pltpu.VMEM((group, rows, n * rows), jnp.bfloat16)],
        ),
        compiler_params=pltpu.CompilerParams(vmem_limit_bytes=48 * 1024 * 1024),
        cost_estimate=pl.CostEstimate(
            flops=0, bytes_accessed=count * 16 * rows * n * half, transcendentals=0
        ),
    )(where, x)


def place(pieces, me, rows, group, spread, other):
    for m in range(group):
        spread[me ^ m] = pieces[m][...].astype(jnp.float32)
    for j in range(group):
        for d in range(2 * group):
            other[d, :, j * rows : (j + 1) * rows] = spread[j, :, d * rows : (d + 1) * rows]


def pack_kernel(rows, group, count, where_ref, x, *refs):
    me, upper = where_ref[0], where_ref[1] == 1
    pieces, out, (spread, other) = refs[:group], refs[group], refs[group + 1 :]
    n, half = 2 * group, rows * group
    b16 = jnp.bfloat16
    f = pl.program_id(0)
    place(pieces, me, rows, group, spread, other)
    mask, diag = pair_mask(rows, group, me * rows, rows)
    base = pl.multiple_of(f * 3 * rows, 16)
    for c in range(2):
        out[:, pl.ds(base + c * rows, rows)] = side(x.at[0, :, c], upper, False).astype(b16)
    re, im = side(x.at[0, :, 0], upper, True), side(x.at[0, :, 1], upper, True)
    keep = jnp.where(mask[None], im, re) + other[...]
    out[:, pl.ds(base + 2 * rows, rows)] = keep.astype(b16)
    line = jnp.sum(jnp.where(diag[None], im, 0.0), axis=1, keepdims=True)
    slot = lax.broadcasted_iota(jnp.int32, (n, TILE, half), 1) == f
    tile = jnp.where(slot, jnp.broadcast_to(line, (n, TILE, half)), 0.0)

    @pl.when(f == 0)
    def _():
        out[:, count * 3 * rows :] = jnp.zeros((n, TILE, half), b16)

    old = out[:, count * 3 * rows :].astype(jnp.float32)
    out[:, count * 3 * rows :] = (old + tile).astype(b16)


def pack(x, pieces, where, rows, group, first, count):
    n, half = 2 * group, rows * group
    shape = (n, count * 3 * rows + TILE, half)
    return pl.pallas_call(
        functools.partial(pack_kernel, rows, group, count),
        out_shape=jax.ShapeDtypeStruct(shape, jnp.bfloat16),
        grid_spec=pltpu.PrefetchScalarGridSpec(
            num_scalar_prefetch=1,
            grid=(count,),
            in_specs=[pl.BlockSpec((1, n, 2, rows, 2 * half), lambda f, w: (f + first, 0, 0, 0, 0))]
            + [pl.BlockSpec((rows, n * rows), lambda f, w: (0, f))] * group,
            out_specs=pl.BlockSpec(shape, lambda f, w: (0, 0, 0)),
            scratch_shapes=[
                pltpu.VMEM((group, rows, n * rows), jnp.float32),
                pltpu.VMEM((n, rows, half), jnp.float32),
            ],
        ),
        compiler_params=pltpu.CompilerParams(vmem_limit_bytes=48 * 1024 * 1024),
        cost_estimate=pl.CostEstimate(
            flops=0, bytes_accessed=count * 20 * rows * n * half, transcendentals=0
        ),
    )(where, x, *pieces)


def unpack_kernel(rows, group, where_ref, re_ref, im_ref, mix_ref, tile_ref, *refs):
    me, upper = where_ref[0], where_ref[1] == 1
    pieces, out, (spread, other) = refs[:group], refs[group], refs[group + 1 :]
    n, half = 2 * group, rows * group
    b16, f32 = jnp.bfloat16, jnp.float32
    f = pl.program_id(0)
    place(pieces, me, rows, group, spread, other)
    mask, diag = pair_mask(rows, group, me * rows, rows)
    slot = lax.broadcasted_iota(jnp.int32, (n, TILE, half), 1) == f
    line = jnp.sum(jnp.where(slot, tile_ref[...].astype(f32), 0.0), axis=1, keepdims=True)
    mix, rest = mix_ref[...].astype(f32), other[...]
    for c, ref in ((0, re_ref), (1, im_ref)):
        if c == 0:
            inner = jnp.where(mask[None], rest, mix)
        else:
            inner = jnp.where(diag[None], line, jnp.where(mask[None], mix, rest))
        outer = ref[...].astype(f32)
        out[:, c, :, :half] = jnp.where(upper, inner, outer).astype(b16)
        out[:, c, :, half:] = jnp.where(upper, outer, inner).astype(b16)


def unpack(back, pieces, where, rows, group, count):
    n, half = 2 * group, rows * group
    last = 3 * rows * count // TILE
    return pl.pallas_call(
        functools.partial(unpack_kernel, rows, group),
        out_shape=jax.ShapeDtypeStruct((count * n, 2, rows, 2 * half), jnp.bfloat16),
        grid_spec=pltpu.PrefetchScalarGridSpec(
            num_scalar_prefetch=1,
            grid=(count,),
            in_specs=[
                pl.BlockSpec((n, rows, half), functools.partial(lambda c, f, w: (0, 3 * f + c, 0), c))
                for c in range(3)
            ]
            + [pl.BlockSpec((n, TILE, half), lambda f, w: (0, last, 0))]
            + [pl.BlockSpec((rows, n * rows), lambda f, w: (0, f))] * group,
            out_specs=pl.BlockSpec((n, 2, rows, 2 * half), lambda f, w: (f, 0, 0, 0)),
            scratch_shapes=[
                pltpu.VMEM((group, rows, n * rows), jnp.float32),
                pltpu.VMEM((n, rows, half), jnp.float32),
            ],
        ),
        compiler_params=pltpu.CompilerParams(vmem_limit_bytes=48 * 1024 * 1024),
        cost_estimate=pl.CostEstimate(
            flops=0, bytes_accessed=count * 20 * rows * n * half, transcendentals=0
        ),
    )(where, *[back] * 4, *pieces)


def swap(pieces, n):
    return list(pieces[:1]) + [
        lax.ppermute(piece, "tile", [(i, i ^ m) for i in range(n)])
        for m, piece in enumerate(pieces)
        if m
    ]


def a2a(x):
    return lax.all_to_all(x, "tile", split_axis=0, concat_axis=0, tiled=True)


def spectrum_of(part, traces):
    return lax.dot_general(
        part, traces, (((part.ndim - 1,), (2,)), ((), ())), preferred_element_type=jnp.float32
    )


def generic(traces, weight, forward, n):
    rows, order = weight.shape
    mirror = lax.all_to_all(
        weight.astype(jnp.bfloat16), "tile", split_axis=1, concat_axis=0, tiled=True
    )
    share = weight / (weight + mirror.T.astype(jnp.float32))
    returned = []
    for chunk in range(NF // n):
        part = forward[chunk * n : (chunk + 1) * n]
        got = a2a((share * spectrum_of(part, traces)).astype(jnp.bfloat16))
        y = [got[:, c].reshape(order, order).astype(jnp.float32) for c in range(2)]
        br, bi = ((v + v.T).astype(jnp.bfloat16) for v in y)
        inv = 1.0 / math.sqrt(order)
        fr, fi = (mm(br, br) - mm(bi, bi)) * inv, (mm(br, bi) + mm(bi, br)) * inv
        gr, gi = (fr - br).astype(jnp.bfloat16), (fi - bi).astype(jnp.bfloat16)
        ar, ai = fr.astype(jnp.bfloat16), fi.astype(jnp.bfloat16)
        parts = [
            fr + (mm(ar, gr) - mm(ai, gi)) * inv,
            fi + (mm(ar, gi) + mm(ai, gr)) * inv,
        ]
        back = jnp.stack([v.astype(jnp.bfloat16).reshape(n, rows, order) for v in parts], 1)
        returned.append(a2a(back))
    return jnp.concatenate(returned, 0)


def pipelined(traces, weight, forward, n):
    order = traces.shape[1]
    rows = traces.shape[0]
    half, group = order // 2, n // 2
    per = NF // n
    b16 = jnp.bfloat16
    index = lax.axis_index("tile")
    where = jnp.stack([index % group, (index < group).astype(jnp.int32)])

    every = lax.all_gather(weight.astype(b16), "tile", axis=0, tiled=True)
    lead = per // 2
    rest = per - lead
    table = forward.reshape(per, n, 2, NT)
    flat = (-1, NT)
    table_in = jnp.concatenate(
        [table[:lead].transpose(1, 0, 2, 3).reshape(flat), table[lead:].reshape(flat)], 0
    )
    table_out = jnp.concatenate(
        [table[:lead].reshape(flat), table[lead:].transpose(1, 0, 2, 3).reshape(flat)], 0
    )
    head, tail = dft(traces, weight, table_in, 2 * lead * n)
    tail = tail.reshape(rest, n, 2, rows, order)
    gifts = give(tail, where, rows, group, 0, rest, True)
    head, gifts = lax.optimization_barrier((head, gifts))
    whole = a2a(head.reshape(n, lead, 2, rows, order))
    packed = pack(tail, swap(gifts, n), where, rows, group, 0, rest)
    packed, every = lax.optimization_barrier((packed, every))
    every = every.astype(jnp.float32)
    ratio = 1.0 / (every + every.T)
    got = a2a(packed)

    parts = [chain(whole, ratio, rows, order, f, 0, f, True) for f in range(lead)]
    tile = sum(part[:, 3 * rows :] for part in parts)
    back = jnp.concatenate([part[:, : 3 * rows] for part in parts] + [tile], 1)
    back, got = lax.optimization_barrier((back, got))
    back = a2a(back)
    parts = [chain(got, ratio, rows, order, f, rest, 0, False) for f in range(rest)]
    parts = jnp.stack(parts, 1)
    gifts = give(back, where, rows, group, 0, lead, False)
    parts, gifts = lax.optimization_barrier((parts, gifts))
    last = a2a(parts)
    full = unpack(back, swap(gifts, n), where, rows, group, lead)
    return idft([part.reshape(-1, rows, order) for part in (full, last)], table_out)


def body(traces, quality):
    rows, order = quality.shape
    n = order // rows
    forward = tables()
    weight = (quality + 1).astype(jnp.float32)
    if rows % 16 == 0 and order % 256 == 0 and n & (n - 1) == 0 and NF // n >= 4:
        return pipelined(traces, weight, forward, n)
    returned = generic(traces, weight, forward, n)
    result = lax.dot_general(
        returned, forward, (((0, 1), (0, 1)), ((), ())), preferred_element_type=jnp.float32
    )
    return result.astype(jnp.bfloat16)


def solution(mesh):
    in_specs = (P(("swath", "tile"), None, None), P(("swath", "tile"), None))
    out_specs = P(("swath", "tile"), None, None)
    return jax.shard_map(body, mesh=mesh, in_specs=in_specs, out_specs=out_specs, check_vma=False)
```

```python
import functools
import math

import jax
import jax.numpy as jnp
from jax import lax
from jax.experimental import pallas as pl
from jax.experimental.pallas import tpu as pltpu
from jax.sharding import PartitionSpec as P

NT = 512
NF = 64
F_LO = 8
TILE = 16


def tables():
    bins = F_LO + jnp.arange(NF, dtype=jnp.int32)
    times = jnp.arange(NT, dtype=jnp.int32)
    phase = bins[:, None] * times[None, :] % NT
    angle = phase.astype(jnp.float32) * jnp.float32(2.0 * math.pi / NT)
    cosine = (jnp.cos(angle) / math.sqrt(NT)).astype(jnp.bfloat16)
    sine = (jnp.sin(angle) / math.sqrt(NT)).astype(jnp.bfloat16)
    return jnp.stack([cosine, -sine], axis=1)


def mm(a, b):
    return jnp.dot(a, b, preferred_element_type=jnp.float32)


def kept(i, j, s, r, group):
    diff = i ^ j
    part = (r > s).astype(jnp.int32)
    bit = 1
    while bit < group:
        part = jnp.where(diff >= bit, (i // bit) % 2, part)
        bit *= 2
    return part == 1


def pair_mask(rows, group, first_row, count):
    s = lax.broadcasted_iota(jnp.int32, (count, rows * group), 0) + first_row
    r = lax.broadcasted_iota(jnp.int32, (count, rows * group), 1)
    return kept(s // rows, r // rows, s, r, group), s == r


def chain_kernel(rows, slot_in, slot_out, packed_in, packed_out, *refs):
    count = 4 if packed_in else 1
    if slot_in is None:
        slot_in = pl.program_id(0)
    ins, ratio, out, (br, bi, fr, fi) = refs[:count], refs[count], refs[count + 1], refs[count + 2 :]
    order = br.shape[0]
    half = order // 2
    n = order // rows
    inv = 1.0 / math.sqrt(order)
    f32, b16 = jnp.float32, jnp.bfloat16
    if packed_in or packed_out:
        mask, diag = pair_mask(rows, n // 2, 0, half)
    if packed_in:
        re, im, mix, extra = ins
        for ref, b in ((re, br), (im, bi)):
            upper = ref[: n // 2].reshape(half, half).astype(f32)
            lower = ref[n // 2 :].reshape(half, half).astype(f32)
            cross = (upper + lower.T) * ratio[:half, half:]
            b[:half, half:] = cross.astype(b16)
            b[half:, :half] = cross.T.astype(b16)
        for h in range(2):
            pick = slice(h * half, (h + 1) * half)
            both = mix[h * (n // 2) : (h + 1) * (n // 2)].reshape(half, half).astype(f32)
            tr = jnp.where(mask, 0.0, both)
            br[pick, pick] = ((tr + tr.T) * ratio[pick, pick]).astype(b16)
            lines = extra[h * (n // 2) : (h + 1) * (n // 2)].astype(f32)
            chosen = lax.broadcasted_iota(jnp.int32, (n // 2, TILE, half), 1) == slot_in
            line = jnp.sum(jnp.sum(jnp.where(chosen, lines, 0.0), axis=0), axis=0, keepdims=True)
            ti = jnp.where(mask, both, 0.0)
            ti = ti + ti.T + jnp.where(diag, 2.0 * line, 0.0)
            bi[pick, pick] = (ti * ratio[pick, pick]).astype(b16)
    else:
        for c, b in ((0, br), (1, bi)):
            y = ins[0][:, 0, c].reshape(order, order).astype(f32)
            b[...] = ((y + y.T) * ratio[...]).astype(b16)
    step = 256 if order % 256 == 0 else order
    for t in range(0, order, step):
        ar, ai = br[t : t + step], bi[t : t + step]
        fr[t : t + step] = (mm(ar, br[...]) - mm(ai, bi[...])) * inv
        fi[t : t + step] = (mm(ar, bi[...]) + mm(ai, br[...])) * inv
    gr = (fr[...] - br[...].astype(f32)).astype(b16)
    gi = (fi[...] - bi[...].astype(f32)).astype(b16)
    br[...] = gr
    bi[...] = gi
    for t in range(0, order, step):
        cr, ci = fr[t : t + step], fi[t : t + step]
        ar, ai = cr.astype(b16), ci.astype(b16)
        pr = cr + (mm(ar, br[...]) - mm(ai, bi[...])) * inv
        pi = ci + (mm(ar, bi[...]) + mm(ai, br[...])) * inv
        fr[t : t + step] = pr
        fi[t : t + step] = pi
    if packed_out:
        out[:, 3 * rows :] = jnp.zeros((n, TILE, half), b16)
        for h in range(2):
            own = slice(h * half, (h + 1) * half)
            other = slice((1 - h) * half, (2 - h) * half)
            dst = slice(h * (n // 2), (h + 1) * (n // 2))
            shape = (n // 2, rows, half)
            out[dst, :rows] = fr[own, other].astype(b16).reshape(shape)
            out[dst, rows : 2 * rows] = fi[own, other].astype(b16).reshape(shape)
            pr, pi = fr[own, own], fi[own, own]
            out[dst, 2 * rows : 3 * rows] = jnp.where(mask, pi, pr).astype(b16).reshape(shape)
            line = jnp.sum(jnp.where(diag, pi, 0.0), axis=0, keepdims=True)
            tile = jnp.where(
                lax.broadcasted_iota(jnp.int32, (TILE, half), 0) == slot_out,
                jnp.broadcast_to(line, (TILE, half)),
                0.0,
            ).astype(b16)
            out[dst, 3 * rows :] = jnp.broadcast_to(tile[None], (n // 2, TILE, half))
    else:
        out[:, 0, 0] = fr[...].astype(b16).reshape(n, rows, order)
        out[:, 0, 1] = fi[...].astype(b16).reshape(n, rows, order)


def chain(got, ratio, rows, order, slot_in, total_in, slot_out, packed_out):
    n, half = order // rows, order // 2
    packed_in = total_in > 0
    if packed_in:
        specs = [
            pl.BlockSpec((n, rows, half), functools.partial(lambda b, i: (0, b, 0), 3 * slot_in + c))
            for c in range(3)
        ]
        last = 3 * rows * total_in // TILE
        specs.append(pl.BlockSpec((n, TILE, half), lambda i: (0, last, 0)))
        args = [got] * 4 + [ratio]
    else:
        specs = [pl.BlockSpec((n, 1, 2, rows, order), lambda i: (0, slot_in, 0, 0, 0))]
        args = [got, ratio]
    specs.append(pl.BlockSpec((order, order), lambda i: (0, 0)))
    shape = (n, 3 * rows + TILE, half) if packed_out else (n, 2, rows, order)
    return pl.pallas_call(
        functools.partial(chain_kernel, rows, slot_in, slot_out, packed_in, packed_out),
        out_shape=jax.ShapeDtypeStruct(shape, jnp.bfloat16),
        grid=(1,),
        in_specs=specs,
        out_specs=pl.BlockSpec(shape, lambda i: (0,) * len(shape)),
        scratch_shapes=[
            pltpu.VMEM((order, order), jnp.bfloat16),
            pltpu.VMEM((order, order), jnp.bfloat16),
            pltpu.VMEM((order, order), jnp.float32),
            pltpu.VMEM((order, order), jnp.float32),
        ],
        compiler_params=pltpu.CompilerParams(vmem_limit_bytes=48 * 1024 * 1024),
        cost_estimate=pl.CostEstimate(
            flops=16 * order**3, bytes_accessed=8 * order * order, transcendentals=0
        ),
    )(*args)


def chain_group(got, ratio, rows, order, count):
    n, half = order // rows, order // 2
    specs = [
        pl.BlockSpec((n, rows, half), functools.partial(lambda c, f: (0, 3 * f + c, 0), c))
        for c in range(3)
    ]
    last = 3 * rows * count // TILE
    specs.append(pl.BlockSpec((n, TILE, half), lambda f: (0, last, 0)))
    specs.append(pl.BlockSpec((order, order), lambda f: (0, 0)))
    return pl.pallas_call(
        functools.partial(chain_kernel, rows, None, 0, True, False),
        out_shape=jax.ShapeDtypeStruct((n, count, 2, rows, order), jnp.bfloat16),
        grid=(count,),
        in_specs=specs,
        out_specs=pl.BlockSpec((n, 1, 2, rows, order), lambda f: (0, f, 0, 0, 0)),
        scratch_shapes=[
            pltpu.VMEM((order, order), jnp.bfloat16),
            pltpu.VMEM((order, order), jnp.bfloat16),
            pltpu.VMEM((order, order), jnp.float32),
            pltpu.VMEM((order, order), jnp.float32),
        ],
        compiler_params=pltpu.CompilerParams(vmem_limit_bytes=48 * 1024 * 1024),
        cost_estimate=pl.CostEstimate(
            flops=16 * count * order**3, bytes_accessed=8 * count * order * order, transcendentals=0
        ),
    )(*[got] * 4, ratio)


def dft_kernel(first, table, weight, traces, head, tail, turn):
    rb, cb = traces.shape[:2]
    count = table.shape[0]
    b16 = jnp.bfloat16
    for s in range(rb):
        lines = lax.dot_general(
            traces[s], table[...], (((1,), (1,)), ((), ())), preferred_element_type=jnp.float32
        ).T
        lines = lines * weight[s : s + 1]
        for c in range(cb // 128):
            turn[c, pl.ds(s, count, stride=rb), :] = lines[:, c * 128 : (c + 1) * 128]
    for c in range(cb // 128):
        pick = slice(c * 128, (c + 1) * 128)
        head[:, :, pick] = turn[c, : first * rb].reshape(first, rb, 128).astype(b16)
        tail[:, :, pick] = turn[c, first * rb :].reshape(count - first, rb, 128).astype(b16)


def dft(traces, weight, table, first):
    rows, order, nt = traces.shape
    count = table.shape[0]
    rb, cb = 16, 384 if order % 384 == 0 else 128
    return pl.pallas_call(
        functools.partial(dft_kernel, first),
        out_shape=[
            jax.ShapeDtypeStruct((first, rows, order), jnp.bfloat16),
            jax.ShapeDtypeStruct((count - first, rows, order), jnp.bfloat16),
        ],
        grid=(rows // rb, order // cb),
        in_specs=[
            pl.BlockSpec((count, nt), lambda i, j: (0, 0)),
            pl.BlockSpec((rb, cb), lambda i, j: (i, j)),
            pl.BlockSpec((rb, cb, nt), lambda i, j: (i, j, 0)),
        ],
        out_specs=[
            pl.BlockSpec((first, rb, cb), lambda i, j: (0, i, j)),
            pl.BlockSpec((count - first, rb, cb), lambda i, j: (0, i, j)),
        ],
        scratch_shapes=[pltpu.VMEM((cb // 128, count * rb, 128), jnp.float32)],
        compiler_params=pltpu.CompilerParams(vmem_limit_bytes=52 * 1024 * 1024),
        cost_estimate=pl.CostEstimate(
            flops=4 * count * rows * order * nt,
            bytes_accessed=2 * rows * order * (nt + count),
            transcendentals=0,
        ),
    )(table, weight, traces)


def idft_kernel(parts, table, *refs):
    ins, out, turn = refs[:parts], refs[parts], refs[parts + 1]
    rb, cb = out.shape[:2]
    count = table.shape[0]
    at = 0
    for ref in ins:
        size = ref.shape[0] * rb
        for c in range(cb // 128):
            piece = ref[:, :, c * 128 : (c + 1) * 128].astype(jnp.float32)
            turn[c, at : at + size] = piece.reshape(size, 128)
        at += size
    for s in range(rb):
        for c in range(cb // 128):
            lines = turn[c, pl.ds(s, count, stride=rb), :].astype(jnp.bfloat16)
            samples = lax.dot_general(
                lines, table[...], (((0,), (0,)), ((), ())), preferred_element_type=jnp.float32
            )
            out[s, c * 128 : (c + 1) * 128] = samples.astype(jnp.bfloat16)


def idft(pieces, table):
    count, nt = table.shape
    rows, order = pieces[0].shape[1:]
    rb, cb = 16, 384 if order % 384 == 0 else 128
    return pl.pallas_call(
        functools.partial(idft_kernel, len(pieces)),
        out_shape=jax.ShapeDtypeStruct((rows, order, nt), jnp.bfloat16),
        grid=(rows // rb, order // cb),
        in_specs=[pl.BlockSpec((count, nt), lambda i, j: (0, 0))]
        + [pl.BlockSpec((piece.shape[0], rb, cb), lambda i, j: (0, i, j)) for piece in pieces],
        out_specs=pl.BlockSpec((rb, cb, nt), lambda i, j: (i, j, 0)),
        scratch_shapes=[pltpu.VMEM((cb // 128, count * rb, 128), jnp.float32)],
        compiler_params=pltpu.CompilerParams(vmem_limit_bytes=52 * 1024 * 1024),
        cost_estimate=pl.CostEstimate(
            flops=4 * count * rows * order * nt,
            bytes_accessed=2 * rows * order * (nt + count),
            transcendentals=0,
        ),
    )(table, *pieces)


def side(ref, upper, inside):
    half = ref.shape[-1] // 2
    low, high = ref[..., :half].astype(jnp.float32), ref[..., half:].astype(jnp.float32)
    return jnp.where(upper == inside, low, high)


def give_kernel(rows, group, whole, where_ref, x, *outs):
    me, upper = where_ref[0], where_ref[1] == 1
    turned = outs[-1]
    n, half = 2 * group, rows * group
    if whole:
        mask, diag = pair_mask(rows, group, me * rows, rows)
        re, im = side(x.at[0, :, 0], upper, True), side(x.at[0, :, 1], upper, True)
        block = jnp.where(diag[None], 0.0, jnp.where(mask[None], re, im))
    else:
        block = x[...].astype(jnp.float32)
    turned[...] = block.reshape(n * rows, half).T.astype(jnp.bfloat16).reshape(group, rows, n * rows)
    for m in range(group):
        outs[m][...] = turned[me ^ m]


def give(x, where, rows, group, first, count, whole):
    n, half = 2 * group, rows * group
    if whole:
        spec = pl.BlockSpec((1, n, 2, rows, 2 * half), lambda f, w: (f + first, 0, 0, 0, 0))
    else:
        spec = pl.BlockSpec((n, rows, half), lambda f, w: (0, 3 * f + 2, 0))
    return pl.pallas_call(
        functools.partial(give_kernel, rows, group, whole),
        out_shape=[jax.ShapeDtypeStruct((rows, count * n * rows), jnp.bfloat16)] * group,
        grid_spec=pltpu.PrefetchScalarGridSpec(
            num_scalar_prefetch=1,
            grid=(count,),
            in_specs=[spec],
            out_specs=[pl.BlockSpec((rows, n * rows), lambda f, w: (0, f))] * group,
            scratch_shapes=[pltpu.VMEM((group, rows, n * rows), jnp.bfloat16)],
        ),
        compiler_params=pltpu.CompilerParams(vmem_limit_bytes=48 * 1024 * 1024),
        cost_estimate=pl.CostEstimate(
            flops=0, bytes_accessed=count * 16 * rows * n * half, transcendentals=0
        ),
    )(where, x)


def place(pieces, me, rows, group, spread, other):
    for m in range(group):
        spread[me ^ m] = pieces[m][...].astype(jnp.float32)
    for j in range(group):
        for d in range(2 * group):
            other[d, :, j * rows : (j + 1) * rows] = spread[j, :, d * rows : (d + 1) * rows]


def pack_kernel(rows, group, count, where_ref, x, *refs):
    me, upper = where_ref[0], where_ref[1] == 1
    pieces, out, (spread, other) = refs[:group], refs[group], refs[group + 1 :]
    n, half = 2 * group, rows * group
    b16 = jnp.bfloat16
    f = pl.program_id(0)
    place(pieces, me, rows, group, spread, other)
    mask, diag = pair_mask(rows, group, me * rows, rows)
    base = pl.multiple_of(f * 3 * rows, 16)
    for c in range(2):
        out[:, pl.ds(base + c * rows, rows)] = side(x.at[0, :, c], upper, False).astype(b16)
    re, im = side(x.at[0, :, 0], upper, True), side(x.at[0, :, 1], upper, True)
    keep = jnp.where(mask[None], im, re) + other[...]
    out[:, pl.ds(base + 2 * rows, rows)] = keep.astype(b16)
    line = jnp.sum(jnp.where(diag[None], im, 0.0), axis=1, keepdims=True)
    slot = lax.broadcasted_iota(jnp.int32, (n, TILE, half), 1) == f
    tile = jnp.where(slot, jnp.broadcast_to(line, (n, TILE, half)), 0.0)

    @pl.when(f == 0)
    def _():
        out[:, count * 3 * rows :] = jnp.zeros((n, TILE, half), b16)

    old = out[:, count * 3 * rows :].astype(jnp.float32)
    out[:, count * 3 * rows :] = (old + tile).astype(b16)


def pack(x, pieces, where, rows, group, first, count):
    n, half = 2 * group, rows * group
    shape = (n, count * 3 * rows + TILE, half)
    return pl.pallas_call(
        functools.partial(pack_kernel, rows, group, count),
        out_shape=jax.ShapeDtypeStruct(shape, jnp.bfloat16),
        grid_spec=pltpu.PrefetchScalarGridSpec(
            num_scalar_prefetch=1,
            grid=(count,),
            in_specs=[pl.BlockSpec((1, n, 2, rows, 2 * half), lambda f, w: (f + first, 0, 0, 0, 0))]
            + [pl.BlockSpec((rows, n * rows), lambda f, w: (0, f))] * group,
            out_specs=pl.BlockSpec(shape, lambda f, w: (0, 0, 0)),
            scratch_shapes=[
                pltpu.VMEM((group, rows, n * rows), jnp.float32),
                pltpu.VMEM((n, rows, half), jnp.float32),
            ],
        ),
        compiler_params=pltpu.CompilerParams(vmem_limit_bytes=48 * 1024 * 1024),
        cost_estimate=pl.CostEstimate(
            flops=0, bytes_accessed=count * 20 * rows * n * half, transcendentals=0
        ),
    )(where, x, *pieces)


def unpack_kernel(rows, group, where_ref, re_ref, im_ref, mix_ref, tile_ref, *refs):
    me, upper = where_ref[0], where_ref[1] == 1
    pieces, out, (spread, other) = refs[:group], refs[group], refs[group + 1 :]
    n, half = 2 * group, rows * group
    b16, f32 = jnp.bfloat16, jnp.float32
    f = pl.program_id(0)
    place(pieces, me, rows, group, spread, other)
    mask, diag = pair_mask(rows, group, me * rows, rows)
    slot = lax.broadcasted_iota(jnp.int32, (n, TILE, half), 1) == f
    line = jnp.sum(jnp.where(slot, tile_ref[...].astype(f32), 0.0), axis=1, keepdims=True)
    mix, rest = mix_ref[...].astype(f32), other[...]
    for c, ref in ((0, re_ref), (1, im_ref)):
        if c == 0:
            inner = jnp.where(mask[None], rest, mix)
        else:
            inner = jnp.where(diag[None], line, jnp.where(mask[None], mix, rest))
        outer = ref[...].astype(f32)
        out[:, c, :, :half] = jnp.where(upper, inner, outer).astype(b16)
        out[:, c, :, half:] = jnp.where(upper, outer, inner).astype(b16)


def unpack(back, pieces, where, rows, group, count):
    n, half = 2 * group, rows * group
    last = 3 * rows * count // TILE
    return pl.pallas_call(
        functools.partial(unpack_kernel, rows, group),
        out_shape=jax.ShapeDtypeStruct((count * n, 2, rows, 2 * half), jnp.bfloat16),
        grid_spec=pltpu.PrefetchScalarGridSpec(
            num_scalar_prefetch=1,
            grid=(count,),
            in_specs=[
                pl.BlockSpec((n, rows, half), functools.partial(lambda c, f, w: (0, 3 * f + c, 0), c))
                for c in range(3)
            ]
            + [pl.BlockSpec((n, TILE, half), lambda f, w: (0, last, 0))]
            + [pl.BlockSpec((rows, n * rows), lambda f, w: (0, f))] * group,
            out_specs=pl.BlockSpec((n, 2, rows, 2 * half), lambda f, w: (f, 0, 0, 0)),
            scratch_shapes=[
                pltpu.VMEM((group, rows, n * rows), jnp.float32),
                pltpu.VMEM((n, rows, half), jnp.float32),
            ],
        ),
        compiler_params=pltpu.CompilerParams(vmem_limit_bytes=48 * 1024 * 1024),
        cost_estimate=pl.CostEstimate(
            flops=0, bytes_accessed=count * 20 * rows * n * half, transcendentals=0
        ),
    )(where, *[back] * 4, *pieces)


def swap(pieces, n):
    return list(pieces[:1]) + [
        lax.ppermute(piece, "tile", [(i, i ^ m) for i in range(n)])
        for m, piece in enumerate(pieces)
        if m
    ]


def a2a(x):
    return lax.all_to_all(x, "tile", split_axis=0, concat_axis=0, tiled=True)


def spectrum_of(part, traces):
    return lax.dot_general(
        part, traces, (((part.ndim - 1,), (2,)), ((), ())), preferred_element_type=jnp.float32
    )


def generic(traces, weight, forward, n):
    rows, order = weight.shape
    mirror = lax.all_to_all(
        weight.astype(jnp.bfloat16), "tile", split_axis=1, concat_axis=0, tiled=True
    )
    share = weight / (weight + mirror.T.astype(jnp.float32))
    returned = []
    for chunk in range(NF // n):
        part = forward[chunk * n : (chunk + 1) * n]
        got = a2a((share * spectrum_of(part, traces)).astype(jnp.bfloat16))
        y = [got[:, c].reshape(order, order).astype(jnp.float32) for c in range(2)]
        br, bi = ((v + v.T).astype(jnp.bfloat16) for v in y)
        inv = 1.0 / math.sqrt(order)
        fr, fi = (mm(br, br) - mm(bi, bi)) * inv, (mm(br, bi) + mm(bi, br)) * inv
        gr, gi = (fr - br).astype(jnp.bfloat16), (fi - bi).astype(jnp.bfloat16)
        ar, ai = fr.astype(jnp.bfloat16), fi.astype(jnp.bfloat16)
        parts = [
            fr + (mm(ar, gr) - mm(ai, gi)) * inv,
            fi + (mm(ar, gi) + mm(ai, gr)) * inv,
        ]
        back = jnp.stack([v.astype(jnp.bfloat16).reshape(n, rows, order) for v in parts], 1)
        returned.append(a2a(back))
    return jnp.concatenate(returned, 0)


def pipelined(traces, weight, forward, n):
    order = traces.shape[1]
    rows = traces.shape[0]
    half, group = order // 2, n // 2
    per = NF // n
    b16 = jnp.bfloat16
    index = lax.axis_index("tile")
    where = jnp.stack([index % group, (index < group).astype(jnp.int32)])

    every = lax.all_gather(weight.astype(b16), "tile", axis=0, tiled=True)
    lead = per // 2
    rest = per - lead
    table = forward.reshape(per, n, 2, NT)
    flat = (-1, NT)
    table_in = jnp.concatenate(
        [table[:lead].transpose(1, 0, 2, 3).reshape(flat), table[lead:].reshape(flat)], 0
    )
    table_out = jnp.concatenate(
        [table[:lead].reshape(flat), table[lead:].transpose(1, 0, 2, 3).reshape(flat)], 0
    )
    head, tail = dft(traces, weight, table_in, 2 * lead * n)
    tail = tail.reshape(rest, n, 2, rows, order)
    gifts = give(tail, where, rows, group, 0, rest, True)
    head, gifts = lax.optimization_barrier((head, gifts))
    whole = a2a(head.reshape(n, lead, 2, rows, order))
    packed = pack(tail, swap(gifts, n), where, rows, group, 0, rest)
    packed, every = lax.optimization_barrier((packed, every))
    every = every.astype(jnp.float32)
    ratio = 1.0 / (every + every.T)
    got = a2a(packed)

    parts = [chain(whole, ratio, rows, order, f, 0, f, True) for f in range(lead)]
    tile = sum(part[:, 3 * rows :] for part in parts)
    back = jnp.concatenate([part[:, : 3 * rows] for part in parts] + [tile], 1)
    back, got = lax.optimization_barrier((back, got))
    back = a2a(back)
    parts = chain_group(got, ratio, rows, order, rest)
    gifts = give(back, where, rows, group, 0, lead, False)
    parts, gifts = lax.optimization_barrier((parts, gifts))
    last = a2a(parts)
    full = unpack(back, swap(gifts, n), where, rows, group, lead)
    return idft([part.reshape(-1, rows, order) for part in (full, last)], table_out)


def body(traces, quality):
    rows, order = quality.shape
    n = order // rows
    forward = tables()
    weight = (quality + 1).astype(jnp.float32)
    if rows % 16 == 0 and order % 256 == 0 and n & (n - 1) == 0 and NF // n >= 4:
        return pipelined(traces, weight, forward, n)
    returned = generic(traces, weight, forward, n)
    result = lax.dot_general(
        returned, forward, (((0, 1), (0, 1)), ((), ())), preferred_element_type=jnp.float32
    )
    return result.astype(jnp.bfloat16)


def solution(mesh):
    in_specs = (P(("swath", "tile"), None, None), P(("swath", "tile"), None))
    out_specs = P(("swath", "tile"), None, None)
    return jax.shard_map(body, mesh=mesh, in_specs=in_specs, out_specs=out_specs, check_vma=False)
```
